512 devices in a mesh: dp: 16 (over x, z_hi, core), tm: 8 (over z_lo), height: 4 (over y).
Axes of the slice: x: 4, y: 4, z: 16 (z_hi: 2, z_lo: 8; z = z_hi * 8 + z_lo), core: 2. Of those that a mesh axis runs over, the one named last changes fastest.
Arguments:
- latent: bfloat16 [256, 8, 16, 512], P(('dp', 'tm'), None, None, 'height'), parts along dimension 0, may hold values from -6 to 6
- gain_latent: float32 [512], P('height'), may hold values from 0.25 to 1.75
- shift_latent: float32 [512], P('height'), may hold values from -3 to 3
- conv_latent: bfloat16 [13824, 512], P('tm', 'height'), may hold values from -0.0546875 to 0.0546875
- up_weight: bfloat16 [512, 2048], P('height'), may hold values from -0.25 to 0.25
- gain_block: float32 [256], replicated, may hold values from 0.25 to 1.75
- shift_block: float32 [256], replicated, may hold values from -3 to 3
- conv_block: bfloat16 [6912, 256], P(('tm', 'height')), may hold values from -0.078125 to 0.078125
- cotangent: bfloat16 [512, 16, 32, 256], P(('dp', 'tm'), 'height'), parts along dimension 0, may hold values from -6 to 6
Outputs:
- decoded: bfloat16 [512, 16, 32, 256], P(('dp', 'tm'), 'height'), parts along dimension 0
- grad_upsampled: bfloat16 [512, 16, 32, 256], P(('dp', 'tm'), 'height'), parts along dimension 0
- grad_weight: float32 [36864, 256], P(('dp', 'tm', 'height')), parts along dimension 0
- grad_gain: float32 [4096], P('dp'), parts along dimension 0
- grad_shift: float32 [4096], P('dp'), parts along dimension 0
The draws below stay inside these ranges and needn't reach their ends.
There are 16 independent parts, one for each index of `dp`. The reference program is written for one: setup_inputs(seed, part) draws one part's arguments, and reference() takes and returns one part's arrays. A program takes and returns all parts, laid end to end along the dimension named above; an argument that names none is the same for every part. Nothing has to cross between parts.
All inputs are finite; a program needn't handle non-finite values.
Results may differ from the reference program's by a relative error of at most 0.009.
Values may be sent and summed in bfloat16 or wider, within the bound.
No kernel may reach another device: no remote copies, remote signals or barrier semaphores. Data moves between devices by JAX's collectives and lax.ppermute only.
A program may use at most 128 MiB of HBM per device.

```python
import jax
import jax.numpy as jnp
from jax import lax

C1 = 512
C2 = 256
GROUPS = 32
W1 = 16
H1 = 8
FRAMES = 16
FRAMES_UP = 32
ROWS_UP = 16
COLS_UP = 32
N_TM = 8
N_HEIGHT = 4


def level_of(rng, shape, pieces, least, high):
    gain = 1.0
    for position, shards_of in pieces:
        steps = jax.random.uniform(jax.random.fold_in(jax.random.fold_in(rng, 6), position), (shards_of,), jnp.float32, least / len(pieces), high / len(pieces))
        gain = gain * jnp.repeat(jnp.exp(steps), shape[position] // shards_of).reshape((-1,) + (1,) * (len(shape) - 1 - position))
    return gain


def noise(own_key, shape, scale, bound, split=(), kind=jnp.bfloat16):
    array = scale * jax.random.normal(own_key, shape, jnp.float32)
    if split:
        array = array * level_of(own_key, shape, split, -0.22, 0.18)
    return jnp.clip(array, -bound, bound).astype(kind)


def setup_inputs(seed: int = 0, part: int = 0) -> dict:
    streams_of = jax.random.split(jax.random.key(seed), 10)
    part_keys = jax.random.split(jax.random.fold_in(streams_of[9], part), 10)
    return {
        "latent": noise(part_keys[0], (FRAMES, H1, W1, C1), 1.0, 6.0, ((0, 8), (3, 4))),
        "gain_latent": jnp.clip(1.0 + 0.15 * jax.random.normal(streams_of[1], (C1,), jnp.float32), 0.25, 1.75),
        "shift_latent": noise(streams_of[2], (C1,), 0.5, 3.0, ((0, 4),), jnp.float32),
        "conv_latent": noise(streams_of[3], (27 * C1, C1), (27 * C1) ** -0.5, 0.0546875, ((0, 8), (1, 4))),
        "up_weight": noise(streams_of[4], (C1, 8 * C2), C1 ** -0.5, 0.25, ((0, 4),)),
        "gain_block": jnp.clip(1.0 + 0.15 * jax.random.normal(streams_of[5], (C2,), jnp.float32), 0.25, 1.75),
        "shift_block": noise(streams_of[6], (C2,), 0.5, 3.0, (), jnp.float32),
        "conv_block": noise(streams_of[7], (27 * C2, C2), (27 * C2) ** -0.5, 0.078125, ((0, 32),)),
        "cotangent": noise(part_keys[8], (FRAMES_UP, ROWS_UP, COLS_UP, C2), 1.0, 6.0, ((0, 8), (1, 4))),
    }


epsilon = 1e-06

def moments(values, groups):
    grouped = values.reshape(-1, groups, values.shape[-1] // groups)
    count_cells = grouped.shape[0] * grouped.shape[2]
    mean_value = lax.optimization_barrier(jnp.sum(grouped, axis=(0, 2))) / count_cells
    mean_square = lax.optimization_barrier(jnp.sum(grouped * grouped, axis=(0, 2))) / count_cells
    inverse = lax.rsqrt(mean_square - mean_value * mean_value + epsilon)
    return (mean_value, inverse)

def standardize(values, mean_value, inverse, groups):
    shape_full = values.shape
    grouped = values.reshape(shape_full[:-1] + (groups, shape_full[-1] // groups))
    return ((grouped - mean_value[:, None]) * inverse[:, None]).reshape(shape_full)

def causal_taps(padded, weight, frames, rows, cols):
    channels_in = padded.shape[-1]
    summed = jnp.zeros((frames * rows * cols, weight.shape[1]), jnp.float32)
    for lag_step in range(3):
        for row_step in range(3):
            for col_step in range(3):
                tap_index = (lag_step * 3 + row_step) * 3 + col_step
                window = padded[lag_step:lag_step + frames, row_step:row_step + rows, col_step:col_step + cols]
                kernel = weight[tap_index * channels_in:(tap_index + 1) * channels_in]
                summed = summed + jnp.dot(window.reshape(-1, channels_in), kernel, preferred_element_type=jnp.float32)
    return summed.reshape(frames, rows, cols, weight.shape[1])

def transposed_taps(padded, weight, frames, rows, cols):
    channels_out = padded.shape[-1]
    channels_in = weight.shape[0] // 27
    summed = jnp.zeros((frames * rows * cols, channels_in), jnp.float32)
    for lag_step in range(3):
        for row_step in range(3):
            for col_step in range(3):
                tap_index = (lag_step * 3 + row_step) * 3 + col_step
                window = padded[2 - lag_step:2 - lag_step + frames, 2 - row_step:2 - row_step + rows, 2 - col_step:2 - col_step + cols]
                kernel = weight[tap_index * channels_in:(tap_index + 1) * channels_in]
                summed = summed + lax.dot_general(window.reshape(-1, channels_out), kernel, (((1,), (1,)), ((), ())), preferred_element_type=jnp.float32)
    return summed.reshape(frames, rows, cols, channels_in)

def weight_terms(padded, grads, frames, rows, cols):
    channels_in = padded.shape[-1]
    flat_grads = grads.reshape(-1, grads.shape[-1])
    blocks = []
    for row_step in range(3):
        for col_step in range(3):
            window = padded[2:2 + frames, row_step:row_step + rows, col_step:col_step + cols]
            blocks.append(lax.dot_general(window.reshape(-1, channels_in), flat_grads, (((0,), (0,)), ((), ())), preferred_element_type=jnp.float32))
    return jnp.concatenate(blocks, 0)

def reference(latent, gain_latent, shift_latent, conv_latent, up_weight, gain_block, shift_block, conv_block, cotangent):
    latent_f32 = latent.astype(jnp.float32)
    mean_latent, inverse_latent = moments(latent_f32, GROUPS)
    normed = standardize(latent_f32, mean_latent, inverse_latent, GROUPS) * gain_latent + shift_latent
    active = jax.nn.silu(normed).astype(jnp.bfloat16)
    frames_latent, rows_latent, cols_latent = (latent.shape[0], latent.shape[1], latent.shape[2])
    padded = jnp.pad(active, ((2, 0), (1, 1), (1, 1), (0, 0)))
    mixed = causal_taps(padded, conv_latent, frames_latent, rows_latent, cols_latent)
    refined = (latent_f32 + mixed).astype(jnp.bfloat16)
    expanded = jnp.dot(refined.reshape(-1, C1), up_weight, preferred_element_type=jnp.float32)
    spread = expanded.reshape(frames_latent, rows_latent, cols_latent, 2, 2, 2, C2)
    spread = spread.transpose(0, 3, 1, 4, 2, 5, 6)
    upsampled = spread.reshape(2 * frames_latent, 2 * rows_latent, 2 * cols_latent, C2).astype(jnp.bfloat16)
    frames_block, rows_block, cols_block = (upsampled.shape[0], upsampled.shape[1], upsampled.shape[2])
    up_f32 = upsampled.astype(jnp.float32)
    mean_block, inverse_block = moments(up_f32, GROUPS)
    standard = standardize(up_f32, mean_block, inverse_block, GROUPS)
    normed_block = standard * gain_block + shift_block
    active_block = jax.nn.silu(normed_block).astype(jnp.bfloat16)
    padded_block = jnp.pad(active_block, ((2, 0), (1, 1), (1, 1), (0, 0)))
    mixed_block = causal_taps(padded_block, conv_block, frames_block, rows_block, cols_block)
    decoded = (up_f32 + mixed_block).astype(jnp.bfloat16)
    grad_padded = jnp.pad(cotangent, ((0, 2), (1, 1), (1, 1), (0, 0)))
    grad_active = transposed_taps(grad_padded, conv_block, frames_block, rows_block, cols_block)
    frames_dev = frames_block // N_TM
    rows_dev = rows_block // N_HEIGHT
    zero_index = jnp.zeros((), jnp.int32)

    def add_device(carried, device):
        time_start = device // N_HEIGHT * frames_dev
        row_start = device % N_HEIGHT * rows_dev
        region = lax.dynamic_slice(padded_block, (time_start, row_start, zero_index, zero_index), (frames_dev + 2, rows_dev + 2, cols_block + 2, C2))
        grads = lax.dynamic_slice(cotangent, (time_start, row_start, zero_index, zero_index), (frames_dev, rows_dev, cols_block, C2))
        term = weight_terms(region, grads, frames_dev, rows_dev, cols_block)
        return (carried + term, None)
    grad_weight, unused = lax.scan(add_device, jnp.zeros((9 * C2, C2), jnp.float32), jnp.arange(N_TM * N_HEIGHT, dtype=jnp.int32))
    sigmoid = jax.nn.sigmoid(normed_block)
    grad_normed = grad_active * sigmoid * (1.0 + normed_block * (1.0 - sigmoid))
    flat_grad = grad_normed.reshape(-1, C2)
    flat_standard = standard.reshape(-1, C2)
    grad_shift = lax.optimization_barrier(jnp.sum(flat_grad, axis=0))
    grad_gain = lax.optimization_barrier(jnp.sum(flat_grad * flat_standard, axis=0))
    per_block = C2 // GROUPS
    count_block = flat_grad.shape[0] * per_block
    first_mean = lax.optimization_barrier(jnp.sum((gain_block * grad_shift).reshape(GROUPS, per_block), axis=1)) / count_block
    second_mean = lax.optimization_barrier(jnp.sum((gain_block * grad_gain).reshape(GROUPS, per_block), axis=1)) / count_block
    grouped_grad = (grad_normed * gain_block).reshape(-1, GROUPS, per_block)
    grouped_standard = standard.reshape(-1, GROUPS, per_block)
    corrected = (grouped_grad - first_mean[:, None] - grouped_standard * second_mean[:, None]) * inverse_block[:, None]
    grad_upsampled = (cotangent.astype(jnp.float32) + corrected.reshape(cotangent.shape)).astype(jnp.bfloat16)
    return (decoded, grad_upsampled, grad_weight, grad_gain, grad_shift)
```

```python
import jax
import jax.numpy as jnp
from jax import lax
from jax.experimental import pallas as pl
from jax.experimental.pallas import tpu as pltpu
from jax.sharding import Mesh, PartitionSpec as P

EPS = 1e-6
BF = jnp.bfloat16
F32 = jnp.float32
VM = pl.BlockSpec(memory_space=pltpu.VMEM)
SM = pl.BlockSpec(memory_space=pltpu.SMEM)
HB = pl.BlockSpec(memory_space=pl.ANY)
PARAMS = pltpu.CompilerParams(vmem_limit_bytes=50 * 1024 * 1024)


def dot(a, b, precision=None):
    return jnp.dot(a, b, preferred_element_type=F32, precision=precision)


def sigmoid(v):
    return 0.5 * jnp.tanh(0.5 * v) + 0.5


def group_matrix(channels, per_group):
    rows = lax.broadcasted_iota(jnp.int32, (channels, channels), 0) // per_group
    cols = lax.broadcasted_iota(jnp.int32, (channels, channels), 1) // per_group
    return jnp.where(rows == cols, 1.0, 0.0).astype(F32)


def group_sums(sums, per_group):
    return dot(sums, group_matrix(sums.shape[1], per_group), lax.Precision.HIGHEST)


def moved(v, step, cols=16):
    n = v.shape[0]
    col = lax.broadcasted_iota(jnp.int32, v.shape, 0) % cols
    if step < 0:
        return jnp.where(col == 0, 0.0, pltpu.roll(v, 1, 0))
    return jnp.where(col == cols - 1, 0.0, pltpu.roll(v, n - 1, 0))


def latent_sums_kernel(x_ref, gain_ref, shift_ref, out_ref):
    v = x_ref[...].reshape(-1, 128).astype(F32)
    rows = jnp.concatenate(
        [
            jnp.sum(v, axis=0, keepdims=True),
            jnp.sum(v * v, axis=0, keepdims=True),
            gain_ref[...],
            shift_ref[...],
            jnp.zeros((4, 128), F32),
        ],
        axis=0,
    )
    out_ref[...] = jnp.broadcast_to(rows[None], out_ref.shape)


def latent_conv_kernel(meta, lat_ref, stats_ref, mine, other, out_ref, act, w, sem):
    core, t, h = meta[0], meta[1], meta[2]

    def weight_copies(low, high):
        copies = []
        for xi in range(4):
            for ti in range(8):
                at = ti * 1728 + xi * 432
                copies.append(
                    pltpu.make_async_copy(
                        low.at[xi, ti, pl.ds(0, 208)], w.at[pl.ds(at, 208)], sem
                    )
                )
                copies.append(
                    pltpu.make_async_copy(high.at[xi, ti], w.at[pl.ds(at + 208, 224)], sem)
                )
        return copies

    @pl.when(core == 0)
    def _():
        for c in weight_copies(mine, other):
            c.start()

    @pl.when(core == 1)
    def _():
        for c in weight_copies(other, mine):
            c.start()

    frame = lax.broadcasted_iota(jnp.int32, (640, 128), 0) // 128
    inside = frame + 2 * t - 3 >= 0
    zero_row = jnp.zeros((5, 1, 16, 128), BF)
    for j in range(4):
        part = stats_ref[0, j]
        for k in range(1, 8):
            part = part + stats_ref[k, j]
        total = group_sums(part, 16) * (1.0 / 32768.0)
        mean = total[0:1]
        inverse = lax.rsqrt(total[1:2] - mean * mean + EPS)
        v = lat_ref[j].reshape(640, 128).astype(F32)
        normed = (v - mean) * inverse * stats_ref[0, j, 2:3] + stats_ref[0, j, 3:4]
        a = jnp.where(inside, normed * sigmoid(normed), 0.0)
        a = a.astype(BF).astype(F32)
        for dc in range(3):
            s = a if dc == 1 else moved(a, dc - 1)
            act[dc, :, 1:9, :, j * 128 : j * 128 + 128] = s.astype(BF).reshape(5, 8, 16, 128)
            act[dc, :, 0:1, :, j * 128 : j * 128 + 128] = zero_row
            act[dc, :, 9:10, :, j * 128 : j * 128 + 128] = zero_row

    for c in weight_copies(mine, other):
        c.wait()
    acc = lat_ref[h, 2:5].reshape(384, 128).astype(F32)
    total = None
    for lag in range(3):
        for dr in range(3):
            for dc in range(3):
                tap = (lag * 3 + dr) * 3 + dc
                window = act[dc, lag : lag + 3, dr : dr + 8].reshape(384, 512)
                term = dot(window, w[tap * 512 : tap * 512 + 512, :])
                total = term if total is None else total + term
    out_ref[...] = (acc + total).astype(BF).reshape(3, 8, 16, 128)


def upsample_kernel(meta, ref_ref, mine, other, up_ref, sums_ref, w, sem):
    core = meta[0]
    copies = []
    for j in range(4):
        copies.append(
            pltpu.make_async_copy(mine.at[j], w.at[pl.ds(j * 128 + core * 64, 64)], sem)
        )
        copies.append(
            pltpu.make_async_copy(
                other.at[j], w.at[pl.ds(j * 128 + (1 - core) * 64, 64)], sem
            )
        )
    for c in copies:
        c.start()
    for c in copies:
        c.wait()
    x = jnp.concatenate([ref_ref[j].reshape(384, 128) for j in range(4)], axis=1)
    first = jnp.zeros((1, 256), F32)
    second = jnp.zeros((1, 256), F32)
    for p in range(2):
        for q in range(2):
            for s in range(2):
                at = ((p * 2 + q) * 2 + s) * 256
                e = dot(x, w[:, at : at + 256]).astype(BF)
                up_ref[:, p, :, q, s] = e.reshape(3, 8, 16, 256)
                own = e[128:].astype(F32)
                first += jnp.sum(own, axis=0, keepdims=True)
                second += jnp.sum(own * own, axis=0, keepdims=True)
    rows = jnp.concatenate([first, second, jnp.zeros((6, 256), F32)], axis=0)
    sums_ref[...] = jnp.broadcast_to(rows[None], sums_ref.shape)


def grad_active_kernel(meta, cot_ref, w_ref, out_ref, q):
    h = meta[2]
    for row in range(6):
        block = jnp.clip(h + (row + 3) // 4 - 1, 0, 3)
        v = cot_ref[block, :, (row + 3) % 4]
        if row == 0:
            v = jnp.where(h > 0, v, jnp.zeros_like(v))
        if row == 5:
            v = jnp.where(h < 3, v, jnp.zeros_like(v))
        s0, s1 = v[:, 0], v[:, 1]
        q[:, row, 1] = s0
        q[:, row, 2] = s1
        q[:, row, 0] = moved(s1.reshape(96, 256).astype(F32), -1).astype(BF).reshape(6, 16, 256)
        q[:, row, 3] = moved(s0.reshape(96, 256).astype(F32), 1).astype(BF).reshape(6, 16, 256)
    total = None
    for lag in range(3):
        for dr in range(3):
            for dc in range(3):
                tap = (lag * 3 + dr) * 3 + dc
                window = q[2 - lag : 6 - lag, 2 - dr : 6 - dr, 2 - dc : 4 - dc].reshape(512, 256)
                term = lax.dot_general(
                    window,
                    w_ref[tap * 256 : tap * 256 + 256, :],
                    (((1,), (1,)), ((), ())),
                    preferred_element_type=F32,
                )
                total = term if total is None else total + term
    out_ref[...] = total


def block_moments(stats_ref):
    part = stats_ref[0]
    for k in range(1, 8):
        part = part + stats_ref[k]
    total = group_sums(part, 8) * (1.0 / 131072.0)
    mean = total[0:1]
    return mean, lax.rsqrt(total[1:2] - mean * mean + EPS)


def grad_norm_kernel(meta, up_ref, stats_ref, gain_ref, shift_ref, ga_ref, gn_ref, sums_ref):
    h = meta[2]
    mean, inverse = block_moments(stats_ref)
    own = up_ref[2:6, pl.ds(4 * h, 4)].reshape(512, 256).astype(F32)
    standard = (own - mean) * inverse
    normed = standard * gain_ref[...] + shift_ref[...]
    sigma = sigmoid(normed)
    gn = ga_ref[...] * sigma * (1.0 + normed * (1.0 - sigma))
    gn_ref[...] = gn
    rows = jnp.concatenate(
        [
            jnp.sum(gn, axis=0, keepdims=True),
            jnp.sum(gn * standard, axis=0, keepdims=True),
            jnp.zeros((6, 256), F32),
        ],
        axis=0,
    )
    sums_ref[...] = jnp.broadcast_to(rows[None], sums_ref.shape)


def weight_grad_kernel(
    meta, up_ref, stats_ref, gain_ref, shift_ref, cot_ref, gw_ref, q_ref, full
):
    t, h = meta[1], meta[2]
    mean, inverse = block_moments(stats_ref)
    scale = inverse * gain_ref[...]
    offset = shift_ref[...] - mean * scale
    q_ref[:, 0:1] = jnp.zeros((6, 1, 4, 16, 256), BF)
    q_ref[:, 17:18] = jnp.zeros((6, 1, 4, 16, 256), BF)
    for f in range(6):
        for s in range(2):
            v = up_ref[f, :, s].reshape(256, 256).astype(F32)
            normed = v * scale + offset
            a = normed * sigmoid(normed)
            if f < 2:
                a = jnp.where(t > 0, a, 0.0)
            a = a.astype(BF)
            a32 = a.astype(F32)
            q_ref[f, 1:17, 1 + s] = a.reshape(16, 16, 256)
            side = moved(a32, 1 if s == 0 else -1).astype(BF).reshape(16, 16, 256)
            q_ref[f, 1:17, 3 if s == 0 else 0] = side
    for dr in range(3):
        for dc in range(3):
            window = q_ref[2:6, dr : dr + 16, dc : dc + 2].reshape(2048, 256)
            g = dot(cot_ref[...], window)
            at = (dr * 3 + dc) * 256
            full[at : at + 256, :] = g.T
    for k in range(8):
        gw_ref[k] = full[pl.ds(pl.multiple_of(k * 288 + h * 72, 8), 72), :].astype(BF)


def interleave(scratch, v):
    for half in range(2):
        for s in range(2):
            part = v[:, s, :, half * 128 : half * 128 + 128]
            scratch[half, :, pl.ds(s, 16, stride=2), :] = part
    return jnp.concatenate([scratch[0], scratch[1]], axis=-1)


def decode_kernel(meta, up_ref, q_ref, w_ref, out_ref, scratch):
    h = meta[2]
    total = up_ref[2:6, pl.ds(4 * h, 4)].reshape(512, 256).astype(F32)
    conv = None
    for lag in range(3):
        for dr in range(3):
            for dc in range(3):
                tap = (lag * 3 + dr) * 3 + dc
                window = q_ref[lag : lag + 4, pl.ds(4 * h + dr, 4), dc : dc + 2].reshape(512, 256)
                term = dot(window, w_ref[tap * 256 : tap * 256 + 256, :])
                conv = term if conv is None else conv + term
    mixed = interleave(scratch, (total + conv).reshape(16, 2, 16, 256))
    out_ref[...] = mixed.astype(BF).reshape(4, 4, 32, 256)


def final_kernel(
    meta, up_ref, stats_ref, gain_ref, sums_ref, gn_ref, cot_ref, out_ref, totals_ref, scratch
):
    h = meta[2]
    mean, inverse = block_moments(stats_ref)
    total = sums_ref[0]
    for k in range(1, 32):
        total = total + sums_ref[k]
    totals_ref[...] = total
    gain = gain_ref[...]
    means = group_sums(total * gain, 8) * (1.0 / 131072.0)
    own = up_ref[2:6, pl.ds(4 * h, 4)].reshape(512, 256).astype(F32)
    standard = (own - mean) * inverse
    corrected = (gn_ref[...] * gain - means[0:1] - standard * means[1:2]) * inverse
    corrected = interleave(scratch, corrected.reshape(16, 2, 16, 256))
    cot = cot_ref[...].reshape(16, 32, 256).astype(F32)
    out_ref[...] = (cot + corrected).astype(BF).reshape(4, 4, 32, 256)


def gathered(v, axis, n):
    return lax.all_to_all(jnp.broadcast_to(v[None], (n, *v.shape)), axis, 0, 0, tiled=True)


def swapped(v):
    return lax.ppermute(v, "core", [(0, 1), (1, 0)])


def later(v, step):
    return lax.ppermute(v, "tm", [(i, i + step) for i in range(8) if 0 <= i + step < 8])


def struct(shape, dtype):
    return jax.ShapeDtypeStruct(shape, dtype)


def local(
    latent,
    gain_latent,
    shift_latent,
    conv_latent,
    up_weight,
    gain_block,
    shift_block,
    conv_block,
    cotangent,
):
    x, core = lax.axis_index("x"), lax.axis_index("core")
    t, h = lax.axis_index("tm"), lax.axis_index("height")
    meta = jnp.stack([core, t, h, x]).astype(jnp.int32)
    gain2, shift2 = gain_block[None], shift_block[None]

    piece = lax.dynamic_slice(conv_latent, (x * 432 + core * 208, 0), (224, 128))
    lat_w = gathered(gathered(piece, "tm", 8), "x", 4)
    lat_w_other = swapped(lat_w)

    sums = pl.pallas_call(
        latent_sums_kernel,
        out_shape=struct((32, 8, 128), F32),
        in_specs=[VM] * 3,
        out_specs=VM,
        compiler_params=PARAMS,
    )(latent, gain_latent[None], shift_latent[None])
    stats_latent = lax.all_to_all(sums, ("tm", "height"), 0, 0, tiled=True).reshape(8, 4, 8, 128)
    five = jnp.concatenate([later(latent[1:], 2), later(latent, 1), latent], 0)
    lat_all = gathered(five, "height", 4)

    up_piece = lax.dynamic_slice(up_weight, (core * 64, 0), (64, 2048))
    up_w = gathered(up_piece, "height", 4)
    up_w_other = swapped(up_w)

    refined = pl.pallas_call(
        latent_conv_kernel,
        out_shape=struct((3, 8, 16, 128), BF),
        in_specs=[SM, VM, VM, HB, HB],
        out_specs=VM,
        scratch_shapes=[
            pltpu.VMEM((3, 5, 10, 16, 512), BF),
            pltpu.VMEM((13824, 128), BF),
            pltpu.SemaphoreType.DMA,
        ],
        compiler_params=PARAMS,
    )(meta, lat_all, stats_latent, lat_w, lat_w_other)
    refined_all = gathered(refined, "height", 4)

    block_piece = lax.dynamic_slice(conv_block, (x * 54 + core * 27, 0), (27, 256))
    block_w = gathered(gathered(gathered(block_piece, "tm", 8), "height", 4), "x", 4)
    block_other = swapped(block_w)
    pair = jnp.where(core == 0, jnp.stack([block_w, block_other]), jnp.stack([block_other, block_w]))
    weight = pair.transpose(3, 2, 1, 0, 4, 5).reshape(6912, 256)

    phased = cotangent.reshape(4, 4, 16, 2, 256).transpose(0, 1, 3, 2, 4)
    six = jnp.concatenate([phased, later(phased[:2], -1)], 0)
    cot_all = gathered(six, "height", 4)
    cot_t = cot_all[:, :4].transpose(5, 1, 0, 2, 3, 4).reshape(256, 2048)
    grad_active = pl.pallas_call(
        grad_active_kernel,
        out_shape=struct((512, 256), F32),
        in_specs=[SM, VM, VM],
        out_specs=VM,
        scratch_shapes=[pltpu.VMEM((6, 6, 4, 16, 256), BF)],
        compiler_params=PARAMS,
    )(meta, cot_all, weight)

    up, up_sums = pl.pallas_call(
        upsample_kernel,
        out_shape=[struct((3, 2, 8, 2, 2, 16, 256), BF), struct((8, 8, 256), F32)],
        in_specs=[SM, VM, HB, HB],
        out_specs=[VM, VM],
        scratch_shapes=[pltpu.VMEM((512, 2048), BF), pltpu.SemaphoreType.DMA],
        compiler_params=PARAMS,
    )(meta, refined_all, up_w, up_w_other)
    up = up.reshape(6, 16, 2, 16, 256)
    stats_block = lax.all_to_all(up_sums, "tm", 0, 0, tiled=True)

    gn, grad_sums = pl.pallas_call(
        grad_norm_kernel,
        out_shape=[struct((512, 256), F32), struct((32, 8, 256), F32)],
        in_specs=[SM] + [VM] * 5,
        out_specs=[VM, VM],
        compiler_params=PARAMS,
    )(meta, up, stats_block, gain2, shift2, grad_active)
    all_sums = lax.all_to_all(grad_sums, ("tm", "height"), 0, 0, tiled=True)

    gw, q = pl.pallas_call(
        weight_grad_kernel,
        out_shape=[struct((8, 72, 256), BF), struct((6, 18, 4, 16, 256), BF)],
        in_specs=[SM] + [VM] * 5,
        out_specs=[VM, VM],
        scratch_shapes=[pltpu.VMEM((2304, 256), F32)],
        compiler_params=PARAMS,
    )(meta, up, stats_block, gain2, shift2, cot_t)
    gw_all = lax.all_to_all(gw, "tm", 0, 0, tiled=True)
    grad_weight = jnp.sum(gw_all.astype(F32), axis=0)

    decoded = pl.pallas_call(
        decode_kernel,
        out_shape=struct((4, 4, 32, 256), BF),
        in_specs=[SM] + [VM] * 3,
        out_specs=VM,
        scratch_shapes=[pltpu.VMEM((2, 16, 32, 128), F32)],
        compiler_params=PARAMS,
    )(meta, up, q, weight)

    grad_up, totals = pl.pallas_call(
        final_kernel,
        out_shape=[struct((4, 4, 32, 256), BF), struct((8, 256), F32)],
        in_specs=[SM] + [VM] * 6,
        out_specs=[VM, VM],
        scratch_shapes=[pltpu.VMEM((2, 16, 32, 128), F32)],
        compiler_params=PARAMS,
    )(meta, up, stats_block, gain2, all_sums, gn, cotangent)
    return decoded, grad_up, grad_weight, totals[1], totals[0]


def solution(mesh):
    fine = Mesh(
        mesh.devices.reshape(4, 2, 2, 8, 4), ("x", "zh", "core", "tm", "height")
    )
    dp = ("x", "zh", "core")
    return jax.shard_map(
        local,
        mesh=fine,
        in_specs=(
            P((*dp, "tm"), None, None, "height"),
            P("height"),
            P("height"),
            P("tm", "height"),
            P("height", None),
            P(),
            P(),
            P(("tm", "height"), None),
            P((*dp, "tm"), "height", None, None),
        ),
        out_specs=(
            P((*dp, "tm"), "height", None, None),
            P((*dp, "tm"), "height", None, None),
            P((*dp, "tm", "height"), None),
            P(dp),
            P(dp),
        ),
        check_vma=False,
    )
```

```python
import jax
import jax.numpy as jnp
from jax import lax
from jax.experimental import pallas as pl
from jax.experimental.pallas import tpu as pltpu
from jax.sharding import Mesh, PartitionSpec as P

EPS = 1e-6
BF = jnp.bfloat16
F32 = jnp.float32
VM = pl.BlockSpec(memory_space=pltpu.VMEM)
SM = pl.BlockSpec(memory_space=pltpu.SMEM)
HB = pl.BlockSpec(memory_space=pl.ANY)
PARAMS = pltpu.CompilerParams(vmem_limit_bytes=50 * 1024 * 1024)


def dot(a, b, precision=None):
    return jnp.dot(a, b, preferred_element_type=F32, precision=precision)


def sigmoid(v):
    return 0.5 * jnp.tanh(0.5 * v) + 0.5


def transpose_kernel(cot_ref, out_ref):
    for k in range(4):
        out_ref[k] = cot_ref[k, 0:4].reshape(512, 256).astype(F32).T.astype(BF)


def group_matrix(channels, per_group):
    rows = lax.broadcasted_iota(jnp.int32, (channels, channels), 0) // per_group
    cols = lax.broadcasted_iota(jnp.int32, (channels, channels), 1) // per_group
    return jnp.where(rows == cols, 1.0, 0.0).astype(F32)


def group_sums(sums, per_group):
    return dot(sums, group_matrix(sums.shape[1], per_group), lax.Precision.HIGHEST)


def moved(v, step, cols=16):
    n = v.shape[0]
    col = lax.broadcasted_iota(jnp.int32, v.shape, 0) % cols
    if step < 0:
        return jnp.where(col == 0, 0.0, pltpu.roll(v, 1, 0))
    return jnp.where(col == cols - 1, 0.0, pltpu.roll(v, n - 1, 0))


def three_terms(v):
    terms = []
    for k in range(3):
        term = v.astype(BF).astype(F32)
        v = v - term
        terms.append(term)
    return terms


def latent_sums_kernel(x_ref, out_ref):
    v = x_ref[...].reshape(-1, 128).astype(F32)
    rows = jnp.concatenate(
        [
            jnp.sum(v, axis=0, keepdims=True),
            jnp.sum(v * v, axis=0, keepdims=True),
            jnp.zeros((6, 128), F32),
        ],
        axis=0,
    )
    out_ref[...] = jnp.broadcast_to(rows[None], out_ref.shape)


def latent_pack_kernel(x_ref, one_ref, two_ref, stats_ref, gain_ref, shift_ref, out_ref):
    total = stats_ref[0]
    for k in range(1, 8):
        total = total + stats_ref[k]
    terms = []
    for v in (total[0:1], total[1:2], gain_ref[...], shift_ref[...]):
        terms += three_terms(v)
    terms = jnp.concatenate(terms + [jnp.zeros((4, 128), F32)], axis=0).astype(BF)
    for k in range(4):
        out_ref[k, 0:128] = two_ref[...].reshape(128, 128)
        out_ref[k, 128:384] = one_ref[...].reshape(256, 128)
        out_ref[k, 384:640] = x_ref[...].reshape(256, 128)
        out_ref[k, 640:656] = terms


def shard_slots(t, core):
    two = t - 2 * (1 - 2 * core)
    return [v & 7 for v in (t, t + 4, t + 7, t + 3, t + 1, t + 5, two + 8, two + 12)]


def each_core(core, mine, other, copies):
    @pl.when(core == 0)
    def _():
        copies(mine, other)

    @pl.when(core == 1)
    def _():
        copies(other, mine)


def latent_conv_kernel(
    meta, lat_ref, m0, m1, o0, o1, out_ref, act, w, sem
):
    core, t, h, x = meta[0], meta[1], meta[2], meta[3]

    def weight_copies(low, high):
        copies = []
        for side, sources in enumerate((low, high)):
            slots = shard_slots(t, side)
            for hop, source in enumerate(sources):
                for two in range(2):
                    xi = (x + (hop if side == 1 else 4 - hop) + 2 * two) & 3
                    for k in range(8):
                        at = pl.multiple_of(slots[k] * 1728 + xi * 432 + side * 208, 16)
                        size = 208 if side == 0 else 224
                        copies.append(
                            pltpu.make_async_copy(
                                source.at[two, k, pl.ds(0, size)], w.at[pl.ds(at, size)], sem
                            )
                        )
        return copies

    def start(low, high):
        for c in weight_copies(low, high):
            c.start()

    each_core(core, (m0, m1), (o0, o1), start)

    frame = lax.broadcasted_iota(jnp.int32, (640, 128), 0) // 128
    inside = frame + 2 * t - 3 >= 0
    zero_row = jnp.zeros((5, 1, 16, 128), BF)
    for j in range(4):
        lanes = slice(j * 128, j * 128 + 128)
        terms = lat_ref[j, 640:656].astype(F32)
        first, second, gain, shift = (
            terms[k : k + 1] + terms[k + 1 : k + 2] + terms[k + 2 : k + 3] for k in (0, 3, 6, 9)
        )
        part = jnp.concatenate([first, second, jnp.zeros((6, 128), F32)], axis=0)
        total = group_sums(part, 16) * (1.0 / 32768.0)
        mean = total[0:1]
        inverse = lax.rsqrt(total[1:2] - mean * mean + EPS)
        v = lat_ref[j, 0:640].astype(F32)
        normed = (v - mean) * inverse * gain + shift
        a = jnp.where(inside, normed * sigmoid(normed), 0.0)
        a = a.astype(BF).astype(F32)
        for dc in range(3):
            s = a if dc == 1 else moved(a, dc - 1)
            act[dc, :, 1:9, :, lanes] = s.astype(BF).reshape(5, 8, 16, 128)
            act[dc, :, 0:1, :, lanes] = zero_row
            act[dc, :, 9:10, :, lanes] = zero_row

    def wait(low, high):
        for c in weight_copies(low, high):
            c.wait()

    each_core(core, (m0, m1), (o0, o1), wait)
    acc = lat_ref[h, 256:640].astype(F32)
    total = None
    for lag in range(3):
        for dr in range(3):
            for dc in range(3):
                tap = (lag * 3 + dr) * 3 + dc
                window = act[dc, lag : lag + 3, dr : dr + 8].reshape(384, 512)
                term = dot(window, w[tap * 512 : tap * 512 + 512, :])
                total = term if total is None else total + term
    out_ref[...] = (acc + total).astype(BF).reshape(3, 8, 16, 128)


def upsample_kernel(meta, pair, rest, mine, other, up_ref, sums_ref, w, sem):
    core, h = meta[0], meta[2]
    copies = []
    for j in range(4):
        hop, two = (h - j) & 1, ((h - j) >> 1) & 1
        slot = jnp.where(hop == 0, two, jnp.where(core == 0, 2 + two, 3 - two))
        at = slot * 128
        for side, source in ((core, mine), (1 - core, other)):
            rows = pl.ds(pl.multiple_of(at + side * 64, 64), 64)
            copies.append(pltpu.make_async_copy(source.at[j], w.at[rows], sem))
    for c in copies:
        c.start()
    for c in copies:
        c.wait()
    x = jnp.concatenate([r[k].reshape(384, 128) for r in (pair, rest) for k in range(2)], axis=1)
    first = jnp.zeros((1, 256), F32)
    second = jnp.zeros((1, 256), F32)
    for p in range(2):
        for q in range(2):
            for s in range(2):
                at = ((p * 2 + q) * 2 + s) * 256
                e = dot(x, w[:, at : at + 256]).astype(BF)
                up_ref[:, p, :, q, s] = e.reshape(3, 8, 16, 256)
                own = e[128:].astype(F32)
                first += jnp.sum(own, axis=0, keepdims=True)
                second += jnp.sum(own * own, axis=0, keepdims=True)
    rows = jnp.concatenate([first, second, jnp.zeros((6, 256), F32)], axis=0)
    sums_ref[...] = jnp.broadcast_to(rows[None], sums_ref.shape)


def grad_active_kernel(meta, cot_ref, got_ref, out_ref, w_ref, q, edges, sem):
    h = meta[2]
    copies = []
    for core in range(2):
        lanes = pl.ds(core * 128, 128)
        for hi in range(4):
            base = hi * 216 - 8 * (hi % 2)
            for xi in range(4):
                first, size = (32, 32) if xi == 3 else (0, 64)
                to = base + (192 if xi == 3 else xi * 64)
                if hi % 2 == 0 and xi == 3:
                    size = 16
                if hi % 2 == 1 and xi == 0:
                    first, size, to = 16, 48, base + 16
                copies.append(
                    pltpu.make_async_copy(
                        got_ref.at[xi, core, hi, :, pl.ds(first, size)],
                        w_ref.at[:, pl.ds(to, size), lanes],
                        sem,
                    )
                )
            xi, row = (3, 48) if hi % 2 == 0 else (0, 0)
            copies.append(
                pltpu.make_async_copy(
                    got_ref.at[xi, core, hi, :, pl.ds(row, 16)], edges.at[core, hi], sem
                )
            )
    for c in copies:
        c.start()
    for row in range(6):
        block = jnp.clip(h + (row + 3) // 4 - 1, 0, 3)
        v = cot_ref[block, :, (row + 3) % 4]
        if row == 0:
            v = jnp.where(h > 0, v, jnp.zeros_like(v))
        if row == 5:
            v = jnp.where(h < 3, v, jnp.zeros_like(v))
        s0, s1 = v[:, 0], v[:, 1]
        q[:, row, 1] = s0
        q[:, row, 2] = s1
        q[:, row, 0] = moved(s1.reshape(96, 256).astype(F32), -1).astype(BF).reshape(6, 16, 256)
        q[:, row, 3] = moved(s0.reshape(96, 256).astype(F32), 1).astype(BF).reshape(6, 16, 256)
    for c in copies:
        c.wait()
    for core in range(2):
        for pair in range(2):
            edge = edges[core, 2 * pair] + edges[core, 2 * pair + 1]
            at = pair * 432 + 208
            w_ref[:, at : at + 16, core * 128 : core * 128 + 128] = edge
    total = None
    w_flat = w_ref.reshape(6912, 256)
    for lag in range(3):
        for dr in range(3):
            for dc in range(3):
                tap = (lag * 3 + dr) * 3 + dc
                window = q[2 - lag : 6 - lag, 2 - dr : 6 - dr, 2 - dc : 4 - dc].reshape(512, 256)
                term = lax.dot_general(
                    window,
                    w_flat[tap * 256 : tap * 256 + 256, :],
                    (((1,), (1,)), ((), ())),
                    preferred_element_type=F32,
                )
                total = term if total is None else total + term
    out_ref[...] = total


def block_moments(stats_ref):
    part = stats_ref[0]
    for k in range(1, 8):
        part = part + stats_ref[k]
    total = group_sums(part, 8) * (1.0 / 131072.0)
    mean = total[0:1]
    return mean, lax.rsqrt(total[1:2] - mean * mean + EPS)


def grad_norm_kernel(meta, up_ref, stats_ref, gain_ref, shift_ref, ga_ref, gn_ref, sums_ref):
    h = meta[2]
    mean, inverse = block_moments(stats_ref)
    own = up_ref[2:6, pl.ds(4 * h, 4)].reshape(512, 256).astype(F32)
    standard = (own - mean) * inverse
    normed = standard * gain_ref[...] + shift_ref[...]
    sigma = sigmoid(normed)
    gn = ga_ref[...] * sigma * (1.0 + normed * (1.0 - sigma))
    gn_ref[...] = gn
    rows = jnp.concatenate(
        [
            jnp.sum(gn, axis=0, keepdims=True),
            jnp.sum(gn * standard, axis=0, keepdims=True),
            jnp.zeros((6, 256), F32),
        ],
        axis=0,
    )
    sums_ref[...] = jnp.broadcast_to(rows[None], sums_ref.shape)


def pack_kernel(gw_ref, sums_ref, out_ref):
    total = sums_ref[0] + sums_ref[1] + sums_ref[2] + sums_ref[3]
    terms = [term[0:2] for term in three_terms(total)]
    terms = jnp.concatenate(terms + [jnp.zeros((2, 256), F32)], axis=0)
    for k in range(8):
        out_ref[k] = jnp.concatenate([gw_ref[k].astype(F32), terms], axis=0).astype(BF)


def weight_grad_kernel(
    meta, up_ref, stats_ref, gain_ref, shift_ref, cot_ref, gw_ref, q_ref, full
):
    t, h = meta[1], meta[2]
    mean, inverse = block_moments(stats_ref)
    scale = inverse * gain_ref[...]
    offset = shift_ref[...] - mean * scale
    q_ref[:, 0:1] = jnp.zeros((6, 1, 4, 16, 256), BF)
    q_ref[:, 17:18] = jnp.zeros((6, 1, 4, 16, 256), BF)
    for f in range(6):
        for s in range(2):
            v = up_ref[f, :, s].reshape(256, 256).astype(F32)
            normed = v * scale + offset
            a = normed * sigmoid(normed)
            if f < 2:
                a = jnp.where(t > 0, a, 0.0)
            a = a.astype(BF)
            a32 = a.astype(F32)
            q_ref[f, 1:17, 1 + s] = a.reshape(16, 16, 256)
            side = moved(a32, 1 if s == 0 else -1).astype(BF).reshape(16, 16, 256)
            q_ref[f, 1:17, 3 if s == 0 else 0] = side
    for dr in range(3):
        for dc in range(3):
            g = None
            for k in range(4):
                window = q_ref[2:6, 4 * k + dr : 4 * k + dr + 4, dc : dc + 2].reshape(512, 256)
                term = dot(cot_ref[k], window)
                g = term if g is None else g + term
            at = (dr * 3 + dc) * 256
            full[at : at + 256, :] = g.T
    for k in range(8):
        gw_ref[k] = full[pl.ds(pl.multiple_of(k * 288 + h * 72, 8), 72), :].astype(BF)


def interleave(scratch, v):
    for half in range(2):
        for s in range(2):
            part = v[:, s, :, half * 128 : half * 128 + 128]
            scratch[half, :, pl.ds(s, 16, stride=2), :] = part
    return jnp.concatenate([scratch[0], scratch[1]], axis=-1)


def decode_kernel(meta, up_ref, q_ref, w_ref, out_ref, scratch):
    h = meta[2]
    total = up_ref[2:6, pl.ds(4 * h, 4)].reshape(512, 256).astype(F32)
    conv = None
    for lag in range(3):
        for dr in range(3):
            for dc in range(3):
                tap = (lag * 3 + dr) * 3 + dc
                window = q_ref[lag : lag + 4, pl.ds(4 * h + dr, 4), dc : dc + 2].reshape(512, 256)
                term = dot(window, w_ref[tap * 256 : tap * 256 + 256, :])
                conv = term if conv is None else conv + term
    mixed = interleave(scratch, (total + conv).reshape(16, 2, 16, 256))
    out_ref[...] = mixed.astype(BF).reshape(4, 4, 32, 256)


def final_kernel(
    meta, up_ref, stats_ref, gain_ref, got_ref, gn_ref, cot_ref, out_ref, gw_ref, totals_ref, scratch
):
    h = meta[2]
    mean, inverse = block_moments(stats_ref)
    got = None
    for k in range(8):
        v = got_ref[k].astype(F32)
        rows = v[72:74] + v[74:76] + v[76:78]
        got = v[0:72] if k == 0 else got + v[0:72]
        total = rows if k == 0 else total + rows
    gw_ref[...] = got
    total = jnp.concatenate([total, jnp.zeros((6, 256), F32)], axis=0)
    totals_ref[...] = total
    gain = gain_ref[...]
    means = group_sums(total * gain, 8) * (1.0 / 131072.0)
    own = up_ref[2:6, pl.ds(4 * h, 4)].reshape(512, 256).astype(F32)
    standard = (own - mean) * inverse
    corrected = (gn_ref[...] * gain - means[0:1] - standard * means[1:2]) * inverse
    corrected = interleave(scratch, corrected.reshape(16, 2, 16, 256))
    cot = cot_ref[...].reshape(16, 32, 256).astype(F32)
    out_ref[...] = (cot + corrected).astype(BF).reshape(4, 4, 32, 256)


def gathered(v, axis, n):
    return lax.all_to_all(jnp.broadcast_to(v[None], (n, *v.shape)), axis, 0, 0, tiled=True)


def swapped(v):
    return lax.ppermute(v, "core", [(0, 1), (1, 0)])


def later(v, step):
    return lax.ppermute(v, "tm", [(i, i + step) for i in range(8) if 0 <= i + step < 8])


def along_z(v, d):
    return lax.ppermute(v, ("zh", "tm"), [(i, (i + d) % 16) for i in range(16)])


def along_z_by_core(v, d):
    pairs = []
    for z in range(16):
        for core in range(2):
            to = (z + (d if core == 0 else -d)) % 16
            pairs.append((((z // 8) * 2 + core) * 8 + z % 8, ((to // 8) * 2 + core) * 8 + to % 8))
    return lax.ppermute(v, ("zh", "core", "tm"), pairs)


def ring_step(v, axis, size, d):
    pairs = []
    for i in range(size):
        for core in range(2):
            to = (i + (d if core == 0 else -d)) % size
            if axis == "x":
                pairs.append((i * 2 + core, to * 2 + core))
            else:
                pairs.append((core * size + i, core * size + to))
    return lax.ppermute(v, ("x", "core") if axis == "x" else ("core", axis), pairs)


def after(v, *others):
    return lax.optimization_barrier((v, *others))[0]


def struct(shape, dtype):
    return jax.ShapeDtypeStruct(shape, dtype)


def call(kernel, out_shape, in_specs, scratch=()):
    several = isinstance(out_shape, list)
    return pl.pallas_call(
        kernel,
        out_shape=out_shape,
        in_specs=in_specs,
        out_specs=[VM] * len(out_shape) if several else VM,
        scratch_shapes=list(scratch),
        compiler_params=PARAMS,
    )


def local(
    latent,
    gain_latent,
    shift_latent,
    conv_latent,
    up_weight,
    gain_block,
    shift_block,
    conv_block,
    cotangent,
):
    x, core = lax.axis_index("x"), lax.axis_index("core")
    t, h = lax.axis_index("tm"), lax.axis_index("height")
    meta = jnp.stack([core, t, h, x]).astype(jnp.int32)
    gain2, shift2 = gain_block[None], shift_block[None]

    piece = lax.dynamic_slice(conv_latent, (x * 432 + core * 208, 0), (224, 128))
    half = lax.dynamic_slice(conv_block, (0, core * 128), (216, 128))
    window = jnp.where(h % 2 == 0, jnp.pad(half, ((0, 8), (0, 0))), jnp.pad(half, ((8, 0), (0, 0))))
    block_piece = lax.dynamic_slice(window, (jnp.minimum(x * 64, 160), 0), (64, 128))
    piece = jnp.concatenate([piece, block_piece])

    sums = call(latent_sums_kernel, struct((8, 8, 128), F32), [VM])(latent)
    stats_latent = lax.all_to_all(sums, "tm", 0, 0, tiled=True)
    two_back, one_back = later(latent[1:], 2), later(latent, 1)

    pair_z = jnp.stack([piece, along_z_by_core(piece, 4)])
    pair_z = after(pair_z, stats_latent, two_back, one_back)
    up_z, down_z, two_z = along_z(pair_z, 1), along_z(pair_z, -1), along_z_by_core(pair_z, 2)
    rows = jnp.concatenate([v[:, :224] for v in (pair_z, up_z, down_z, two_z)])

    near, far = two_z[0, 224:], two_z[1, 224:]
    plus_2, plus_6 = jnp.where(core == 0, far, near), jnp.where(core == 0, near, far)
    steps = [
        pair_z[0, 224:], down_z[0, 224:], plus_2, up_z[1, 224:],
        pair_z[1, 224:], down_z[1, 224:], plus_6, up_z[0, 224:],
    ]
    ordered = lax.dynamic_slice(jnp.stack(steps + steps), ((8 - t) % 8, 0, 0), (8, 64, 128))
    block_w = lax.all_gather(ordered, ("x", "core", "height"))
    block_w = block_w.reshape(4, 2, 4, 8, 64, 128)

    pair_x = jnp.stack([rows, ring_step(rows, "x", 4, 2)])
    lat = call(latent_pack_kernel, struct((4, 656, 128), BF), [VM] * 6)(
        latent, one_back, two_back, stats_latent, gain_latent[None], shift_latent[None]
    )
    lat_all = lax.all_to_all(lat, "height", 0, 0, tiled=True)
    pair_x = after(pair_x, lat_all)
    rest_x = ring_step(pair_x, "x", 4, 1)
    other_pair = swapped(pair_x)

    up_piece = lax.dynamic_slice(up_weight, (core * 64, 0), (64, 2048))
    up_w = gathered(after(up_piece, lat_all), "height", 4)
    phased = cotangent.reshape(4, 4, 16, 2, 256).transpose(0, 1, 3, 2, 4)
    phased = after(phased, lat_all)
    six = jnp.concatenate([phased, later(phased[:2], -1)], 0)
    six = after(six, up_w)
    other_rest = swapped(after(rest_x, up_w, six))

    refined = call(
        latent_conv_kernel,
        struct((3, 8, 16, 128), BF),
        [SM, VM] + [HB] * 4,
        [
            pltpu.VMEM((3, 5, 10, 16, 512), BF),
            pltpu.VMEM((13824, 128), BF),
            pltpu.SemaphoreType.DMA,
        ],
    )(meta, lat_all, pair_x, rest_x, other_pair, other_rest)
    pair_y = jnp.stack([refined, ring_step(refined, "height", 4, 2)])
    rest_y = ring_step(pair_y, "height", 4, 1)

    up_w_other = swapped(after(up_w, refined))
    cot_all = gathered(six, "height", 4)
    cot_t = call(transpose_kernel, struct((4, 256, 512), BF), [VM])(cot_all)
    grad_active, weight = call(
        grad_active_kernel,
        [struct((512, 256), F32), struct((8, 864, 256), BF)],
        [SM, VM, HB],
        [
            pltpu.VMEM((6, 6, 4, 16, 256), BF),
            pltpu.VMEM((2, 4, 8, 16, 128), BF),
            pltpu.SemaphoreType.DMA,
        ],
    )(meta, after(cot_all, cot_t), block_w)
    weight = weight.reshape(6912, 256)

    up, up_sums = call(
        upsample_kernel,
        [struct((3, 2, 8, 2, 2, 16, 256), BF), struct((8, 8, 256), F32)],
        [SM, VM, VM, HB, HB],
        [pltpu.VMEM((512, 2048), BF), pltpu.SemaphoreType.DMA],
    )(meta, pair_y, rest_y, up_w, up_w_other)
    up = up.reshape(6, 16, 2, 16, 256)
    stats_block = lax.all_to_all(up_sums, "tm", 0, 0, tiled=True)

    gn, grad_sums = call(
        grad_norm_kernel, [struct((512, 256), F32), struct((4, 8, 256), F32)], [SM] + [VM] * 5
    )(meta, up, stats_block, gain2, shift2, grad_active)
    all_sums = lax.all_to_all(grad_sums, "height", 0, 0, tiled=True)

    gw, q = call(
        weight_grad_kernel,
        [struct((8, 72, 256), BF), struct((6, 18, 4, 16, 256), BF)],
        [SM] + [VM] * 5,
        [pltpu.VMEM((2304, 256), F32)],
    )(meta, up, stats_block, gain2, shift2, cot_t)
    packed = call(pack_kernel, struct((8, 80, 256), BF), [VM] * 2)(gw, all_sums)
    got = lax.all_to_all(packed, "tm", 0, 0, tiled=True)

    decoded = call(
        decode_kernel,
        struct((4, 4, 32, 256), BF),
        [SM] + [VM] * 3,
        [pltpu.VMEM((2, 16, 32, 128), F32)],
    )(meta, up, q, weight)

    grad_up, grad_weight, totals = call(
        final_kernel,
        [struct((4, 4, 32, 256), BF), struct((72, 256), F32), struct((8, 256), F32)],
        [SM] + [VM] * 6,
        [pltpu.VMEM((2, 16, 32, 128), F32)],
    )(meta, up, stats_block, gain2, got, gn, cotangent)
    return decoded, grad_up, grad_weight, totals[1], totals[0]


def solution(mesh):
    fine = Mesh(
        mesh.devices.reshape(4, 2, 2, 8, 4), ("x", "zh", "core", "tm", "height")
    )
    dp = ("x", "zh", "core")
    return jax.shard_map(
        local,
        mesh=fine,
        in_specs=(
            P((*dp, "tm"), None, None, "height"),
            P("height"),
            P("height"),
            P("tm", "height"),
            P("height", None),
            P(),
            P(),
            P(("tm", "height"), None),
            P((*dp, "tm"), "height", None, None),
        ),
        out_specs=(
            P((*dp, "tm"), "height", None, None),
            P((*dp, "tm"), "height", None, None),
            P((*dp, "tm", "height"), None),
            P(dp),
            P(dp),
        ),
        check_vma=False,
    )
```

```python
import jax
import jax.numpy as jnp
from jax import lax
from jax.experimental import pallas as pl
from jax.experimental.pallas import tpu as pltpu
from jax.sharding import Mesh, PartitionSpec as P

EPS = 1e-6
BF = jnp.bfloat16
F32 = jnp.float32
VM = pl.BlockSpec(memory_space=pltpu.VMEM)
SM = pl.BlockSpec(memory_space=pltpu.SMEM)
HB = pl.BlockSpec(memory_space=pl.ANY)
PARAMS = pltpu.CompilerParams(vmem_limit_bytes=50 * 1024 * 1024)


def dot(a, b, precision=None):
    return jnp.dot(a, b, preferred_element_type=F32, precision=precision)


def sigmoid(v):
    return 0.5 * jnp.tanh(0.5 * v) + 0.5


def transpose_kernel(meta, pair, rest, out_ref):
    core, h = meta[0], meta[2]
    side = 2 * core - 1
    for k, slot in enumerate((pair.at[0], pair.at[1], rest.at[0], rest.at[1])):
        j = (h + 2 * k if k < 2 else h + side * (2 * k - 3)) & 3
        out_ref[j] = slot[0:4].reshape(512, 256).astype(F32).T.astype(BF)


def group_matrix(channels, per_group):
    rows = lax.broadcasted_iota(jnp.int32, (channels, channels), 0) // per_group
    cols = lax.broadcasted_iota(jnp.int32, (channels, channels), 1) // per_group
    return jnp.where(rows == cols, 1.0, 0.0).astype(F32)


def group_sums(sums, per_group):
    return dot(sums, group_matrix(sums.shape[1], per_group), lax.Precision.HIGHEST)


def moved(v, step, cols=16):
    n = v.shape[0]
    col = lax.broadcasted_iota(jnp.int32, v.shape, 0) % cols
    if step < 0:
        return jnp.where(col == 0, 0.0, pltpu.roll(v, 1, 0))
    return jnp.where(col == cols - 1, 0.0, pltpu.roll(v, n - 1, 0))


def three_terms(v):
    terms = []
    for k in range(3):
        term = v.astype(BF).astype(F32)
        v = v - term
        terms.append(term)
    return terms


def latent_sums_kernel(x_ref, out_ref):
    v = x_ref[...].reshape(-1, 128).astype(F32)
    rows = jnp.concatenate(
        [
            jnp.sum(v, axis=0, keepdims=True),
            jnp.sum(v * v, axis=0, keepdims=True),
            jnp.zeros((6, 128), F32),
        ],
        axis=0,
    )
    out_ref[...] = jnp.broadcast_to(rows[None], out_ref.shape)


def latent_pack_kernel(x_ref, one_ref, two_ref, stats_ref, gain_ref, shift_ref, out_ref):
    total = stats_ref[0]
    for k in range(1, 8):
        total = total + stats_ref[k]
    terms = []
    for v in (total[0:1], total[1:2], gain_ref[...], shift_ref[...]):
        terms += three_terms(v)
    terms = jnp.concatenate(terms + [jnp.zeros((4, 128), F32)], axis=0).astype(BF)
    for k in range(4):
        out_ref[k, 0:128] = two_ref[...].reshape(128, 128)
        out_ref[k, 128:384] = one_ref[...].reshape(256, 128)
        out_ref[k, 384:640] = x_ref[...].reshape(256, 128)
        out_ref[k, 640:656] = terms


def shard_slots(t, core):
    two = t - 2 * (1 - 2 * core)
    return [v & 7 for v in (t, t + 4, t + 7, t + 3, t + 1, t + 5, two + 8, two + 12)]


def each_core(core, mine, other, copies):
    @pl.when(core == 0)
    def _():
        copies(mine, other)

    @pl.when(core == 1)
    def _():
        copies(other, mine)


def latent_conv_kernel(
    meta, lat_ref, m0, m1, o0, o1, out_ref, act, w, sem
):
    core, t, h, x = meta[0], meta[1], meta[2], meta[3]

    def weight_copies(low, high):
        copies = []
        for side, sources in enumerate((low, high)):
            slots = shard_slots(t, side)
            for hop, source in enumerate(sources):
                for two in range(2):
                    xi = (x + (hop if side == 1 else 4 - hop) + 2 * two) & 3
                    for k in range(8):
                        at = pl.multiple_of(slots[k] * 1728 + xi * 432 + side * 208, 16)
                        size = 208 if side == 0 else 224
                        copies.append(
                            pltpu.make_async_copy(
                                source.at[two, k, pl.ds(0, size)], w.at[pl.ds(at, size)], sem
                            )
                        )
        return copies

    def start(low, high):
        for c in weight_copies(low, high):
            c.start()

    each_core(core, (m0, m1), (o0, o1), start)

    frame = lax.broadcasted_iota(jnp.int32, (640, 128), 0) // 128
    inside = frame + 2 * t - 3 >= 0
    zero_row = jnp.zeros((5, 1, 16, 128), BF)
    for j in range(4):
        lanes = slice(j * 128, j * 128 + 128)
        terms = lat_ref[j, 640:656].astype(F32)
        first, second, gain, shift = (
            terms[k : k + 1] + terms[k + 1 : k + 2] + terms[k + 2 : k + 3] for k in (0, 3, 6, 9)
        )
        part = jnp.concatenate([first, second, jnp.zeros((6, 128), F32)], axis=0)
        total = group_sums(part, 16) * (1.0 / 32768.0)
        mean = total[0:1]
        inverse = lax.rsqrt(total[1:2] - mean * mean + EPS)
        v = lat_ref[j, 0:640].astype(F32)
        normed = (v - mean) * inverse * gain + shift
        a = jnp.where(inside, normed * sigmoid(normed), 0.0)
        a = a.astype(BF).astype(F32)
        for dc in range(3):
            s = a if dc == 1 else moved(a, dc - 1)
            act[dc, :, 1:9, :, lanes] = s.astype(BF).reshape(5, 8, 16, 128)
            act[dc, :, 0:1, :, lanes] = zero_row
            act[dc, :, 9:10, :, lanes] = zero_row

    def wait(low, high):
        for c in weight_copies(low, high):
            c.wait()

    each_core(core, (m0, m1), (o0, o1), wait)
    acc = lat_ref[h, 256:640].astype(F32)
    total = None
    for lag in range(3):
        for dr in range(3):
            for dc in range(3):
                tap = (lag * 3 + dr) * 3 + dc
                window = act[dc, lag : lag + 3, dr : dr + 8].reshape(384, 512)
                term = dot(window, w[tap * 512 : tap * 512 + 512, :])
                total = term if total is None else total + term
    refined = (acc + total).astype(BF).reshape(3, 8, 16, 128)
    for k in range(4):
        out_ref[k] = refined


def upsample_kernel(ref_ref, got_ref, up_ref, sums_ref, w, sem):
    copies = [
        pltpu.make_async_copy(got_ref.at[j], w.at[pl.ds(j * 128, 128)], sem) for j in range(4)
    ]
    for c in copies:
        c.start()
    for c in copies:
        c.wait()
    x = jnp.concatenate([ref_ref[j].reshape(384, 128) for j in range(4)], axis=1)
    first = jnp.zeros((1, 256), F32)
    second = jnp.zeros((1, 256), F32)
    for p in range(2):
        for q in range(2):
            for s in range(2):
                at = ((p * 2 + q) * 2 + s) * 256
                e = dot(x, w[:, at : at + 256]).astype(BF)
                up_ref[:, p, :, q, s] = e.reshape(3, 8, 16, 256)
                own = e[128:].astype(F32)
                first += jnp.sum(own, axis=0, keepdims=True)
                second += jnp.sum(own * own, axis=0, keepdims=True)
    rows = jnp.concatenate([first, second, jnp.zeros((6, 256), F32)], axis=0)
    sums_ref[...] = jnp.broadcast_to(rows[None], sums_ref.shape)


def grad_active_kernel(meta, pair, rest, got_ref, out_ref, w_ref, q, edges, sem):
    own_core, h = meta[0], meta[2]
    copies = []
    for core in range(2):
        lanes = pl.ds(core * 128, 128)
        for hi in range(4):
            base = hi * 216 - 8 * (hi % 2)
            for xi in range(4):
                first, size = (32, 32) if xi == 3 else (0, 64)
                to = base + (192 if xi == 3 else xi * 64)
                if hi % 2 == 0 and xi == 3:
                    size = 16
                if hi % 2 == 1 and xi == 0:
                    first, size, to = 16, 48, base + 16
                copies.append(
                    pltpu.make_async_copy(
                        got_ref.at[xi, core, hi, :, pl.ds(first, size)],
                        w_ref.at[:, pl.ds(to, size), lanes],
                        sem,
                    )
                )
            xi, row = (3, 48) if hi % 2 == 0 else (0, 0)
            copies.append(
                pltpu.make_async_copy(
                    got_ref.at[xi, core, hi, :, pl.ds(row, 16)], edges.at[core, hi], sem
                )
            )
    for c in copies:
        c.start()
    for row in range(6):
        if row == 0:
            v = rest[own_core, :, 3]
        elif row == 5:
            v = rest[1 - own_core, :, 0]
        else:
            v = pair[0, :, row - 1]
        if row == 0:
            v = jnp.where(h > 0, v, jnp.zeros_like(v))
        if row == 5:
            v = jnp.where(h < 3, v, jnp.zeros_like(v))
        s0, s1 = v[:, 0], v[:, 1]
        q[:, row, 1] = s0
        q[:, row, 2] = s1
        q[:, row, 0] = moved(s1.reshape(96, 256).astype(F32), -1).astype(BF).reshape(6, 16, 256)
        q[:, row, 3] = moved(s0.reshape(96, 256).astype(F32), 1).astype(BF).reshape(6, 16, 256)
    for c in copies:
        c.wait()
    for core in range(2):
        for pair in range(2):
            edge = edges[core, 2 * pair] + edges[core, 2 * pair + 1]
            at = pair * 432 + 208
            w_ref[:, at : at + 16, core * 128 : core * 128 + 128] = edge
    total = None
    w_flat = w_ref.reshape(6912, 256)
    for lag in range(3):
        for dr in range(3):
            for dc in range(3):
                tap = (lag * 3 + dr) * 3 + dc
                window = q[2 - lag : 6 - lag, 2 - dr : 6 - dr, 2 - dc : 4 - dc].reshape(512, 256)
                term = lax.dot_general(
                    window,
                    w_flat[tap * 256 : tap * 256 + 256, :],
                    (((1,), (1,)), ((), ())),
                    preferred_element_type=F32,
                )
                total = term if total is None else total + term
    out_ref[...] = total


def block_moments(stats_ref):
    part = stats_ref[0]
    for k in range(1, 8):
        part = part + stats_ref[k]
    total = group_sums(part, 8) * (1.0 / 131072.0)
    mean = total[0:1]
    return mean, lax.rsqrt(total[1:2] - mean * mean + EPS)


def grad_norm_kernel(meta, up_ref, stats_ref, gain_ref, shift_ref, ga_ref, gn_ref, sums_ref):
    h = meta[2]
    mean, inverse = block_moments(stats_ref)
    own = up_ref[2:6, pl.ds(4 * h, 4)].reshape(512, 256).astype(F32)
    standard = (own - mean) * inverse
    normed = standard * gain_ref[...] + shift_ref[...]
    sigma = sigmoid(normed)
    gn = ga_ref[...] * sigma * (1.0 + normed * (1.0 - sigma))
    gn_ref[...] = gn
    rows = jnp.concatenate(
        [
            jnp.sum(gn, axis=0, keepdims=True),
            jnp.sum(gn * standard, axis=0, keepdims=True),
            jnp.zeros((6, 256), F32),
        ],
        axis=0,
    )
    sums_ref[...] = jnp.broadcast_to(rows[None], sums_ref.shape)


def pack_kernel(gw_ref, sums_ref, out_ref):
    total = sums_ref[0] + sums_ref[1] + sums_ref[2] + sums_ref[3]
    terms = [term[0:2] for term in three_terms(total)]
    terms = jnp.concatenate(terms + [jnp.zeros((2, 256), F32)], axis=0)
    for k in range(8):
        out_ref[k] = jnp.concatenate([gw_ref[k].astype(F32), terms], axis=0).astype(BF)


def weight_grad_kernel(
    meta, up_ref, stats_ref, gain_ref, shift_ref, cot_ref, gw_ref, q_ref, full
):
    t, h = meta[1], meta[2]
    mean, inverse = block_moments(stats_ref)
    scale = inverse * gain_ref[...]
    offset = shift_ref[...] - mean * scale
    q_ref[:, 0:1] = jnp.zeros((6, 1, 4, 16, 256), BF)
    q_ref[:, 17:18] = jnp.zeros((6, 1, 4, 16, 256), BF)
    for f in range(6):
        for s in range(2):
            v = up_ref[f, :, s].reshape(256, 256).astype(F32)
            normed = v * scale + offset
            a = normed * sigmoid(normed)
            if f < 2:
                a = jnp.where(t > 0, a, 0.0)
            a = a.astype(BF)
            a32 = a.astype(F32)
            q_ref[f, 1:17, 1 + s] = a.reshape(16, 16, 256)
            side = moved(a32, 1 if s == 0 else -1).astype(BF).reshape(16, 16, 256)
            q_ref[f, 1:17, 3 if s == 0 else 0] = side
    for dr in range(3):
        for dc in range(3):
            g = None
            for k in range(4):
                window = q_ref[2:6, 4 * k + dr : 4 * k + dr + 4, dc : dc + 2].reshape(512, 256)
                term = dot(cot_ref[k], window)
                g = term if g is None else g + term
            at = (dr * 3 + dc) * 256
            full[at : at + 256, :] = g.T
    for k in range(8):
        gw_ref[k] = full[pl.ds(pl.multiple_of(k * 288 + h * 72, 8), 72), :].astype(BF)


def interleave(scratch, v):
    for half in range(2):
        for s in range(2):
            part = v[:, s, :, half * 128 : half * 128 + 128]
            scratch[half, :, pl.ds(s, 16, stride=2), :] = part
    return jnp.concatenate([scratch[0], scratch[1]], axis=-1)


def decode_kernel(meta, up_ref, q_ref, w_ref, out_ref, scratch):
    h = meta[2]
    total = up_ref[2:6, pl.ds(4 * h, 4)].reshape(512, 256).astype(F32)
    conv = None
    for lag in range(3):
        for dr in range(3):
            for dc in range(3):
                tap = (lag * 3 + dr) * 3 + dc
                window = q_ref[lag : lag + 4, pl.ds(4 * h + dr, 4), dc : dc + 2].reshape(512, 256)
                term = dot(window, w_ref[tap * 256 : tap * 256 + 256, :])
                conv = term if conv is None else conv + term
    mixed = interleave(scratch, (total + conv).reshape(16, 2, 16, 256))
    out_ref[...] = mixed.astype(BF).reshape(4, 4, 32, 256)


def final_kernel(
    meta, up_ref, stats_ref, gain_ref, got_ref, gn_ref, cot_ref, out_ref, gw_ref, totals_ref, scratch
):
    h = meta[2]
    mean, inverse = block_moments(stats_ref)
    got = None
    for k in range(8):
        v = got_ref[k].astype(F32)
        rows = v[72:74] + v[74:76] + v[76:78]
        got = v[0:72] if k == 0 else got + v[0:72]
        total = rows if k == 0 else total + rows
    gw_ref[...] = got
    total = jnp.concatenate([total, jnp.zeros((6, 256), F32)], axis=0)
    totals_ref[...] = total
    gain = gain_ref[...]
    means = group_sums(total * gain, 8) * (1.0 / 131072.0)
    own = up_ref[2:6, pl.ds(4 * h, 4)].reshape(512, 256).astype(F32)
    standard = (own - mean) * inverse
    corrected = (gn_ref[...] * gain - means[0:1] - standard * means[1:2]) * inverse
    corrected = interleave(scratch, corrected.reshape(16, 2, 16, 256))
    cot = cot_ref[...].reshape(16, 32, 256).astype(F32)
    out_ref[...] = (cot + corrected).astype(BF).reshape(4, 4, 32, 256)


def gathered(v, axis, n):
    return lax.all_to_all(jnp.broadcast_to(v[None], (n, *v.shape)), axis, 0, 0, tiled=True)


def swapped(v):
    return lax.ppermute(v, "core", [(0, 1), (1, 0)])


def later(v, step):
    return lax.ppermute(v, "tm", [(i, i + step) for i in range(8) if 0 <= i + step < 8])


def along_z(v, d):
    return lax.ppermute(v, ("zh", "tm"), [(i, (i + d) % 16) for i in range(16)])


def along_z_by_core(v, d):
    pairs = []
    for z in range(16):
        for core in range(2):
            to = (z + (d if core == 0 else -d)) % 16
            pairs.append((((z // 8) * 2 + core) * 8 + z % 8, ((to // 8) * 2 + core) * 8 + to % 8))
    return lax.ppermute(v, ("zh", "core", "tm"), pairs)


def ring_step(v, axis, size, d):
    pairs = []
    for i in range(size):
        for core in range(2):
            to = (i + (d if core == 0 else -d)) % size
            if axis == "x":
                pairs.append((i * 2 + core, to * 2 + core))
            else:
                pairs.append((core * size + i, core * size + to))
    return lax.ppermute(v, ("x", "core") if axis == "x" else ("core", axis), pairs)


def after(v, *others):
    return lax.optimization_barrier((v, *others))[0]


def in_hbm(v):
    return pltpu.with_memory_space_constraint(v, pltpu.HBM)


def struct(shape, dtype):
    return jax.ShapeDtypeStruct(shape, dtype)


def call(kernel, out_shape, in_specs, scratch=()):
    several = isinstance(out_shape, list)
    return pl.pallas_call(
        kernel,
        out_shape=out_shape,
        in_specs=in_specs,
        out_specs=[VM] * len(out_shape) if several else VM,
        scratch_shapes=list(scratch),
        compiler_params=PARAMS,
    )


def local(
    latent,
    gain_latent,
    shift_latent,
    conv_latent,
    up_weight,
    gain_block,
    shift_block,
    conv_block,
    cotangent,
):
    x, core = lax.axis_index("x"), lax.axis_index("core")
    t, h = lax.axis_index("tm"), lax.axis_index("height")
    meta = jnp.stack([core, t, h, x]).astype(jnp.int32)
    gain2, shift2 = gain_block[None], shift_block[None]

    up_w = lax.all_gather(up_weight, "height")

    piece = lax.dynamic_slice(conv_latent, (x * 432 + core * 208, 0), (224, 128))
    half = lax.dynamic_slice(conv_block, (0, core * 128), (216, 128))
    window = jnp.where(h % 2 == 0, jnp.pad(half, ((0, 8), (0, 0))), jnp.pad(half, ((8, 0), (0, 0))))
    block_piece = lax.dynamic_slice(window, (jnp.minimum(x * 64, 160), 0), (64, 128))
    piece = jnp.concatenate([piece, block_piece])

    sums = call(latent_sums_kernel, struct((8, 8, 128), F32), [VM])(latent)
    stats_latent = lax.all_to_all(sums, "tm", 0, 0, tiled=True)
    two_back, one_back = later(latent[1:], 2), later(latent, 1)

    pair_z = jnp.stack([piece, along_z_by_core(piece, 4)])
    pair_z = after(pair_z, stats_latent, two_back, one_back)
    up_z, down_z, two_z = along_z(pair_z, 1), along_z(pair_z, -1), along_z_by_core(pair_z, 2)
    rows = jnp.concatenate([v[:, :224] for v in (pair_z, up_z, down_z, two_z)])

    near, far = two_z[0, 224:], two_z[1, 224:]
    plus_2, plus_6 = jnp.where(core == 0, far, near), jnp.where(core == 0, near, far)
    steps = [
        pair_z[0, 224:], down_z[0, 224:], plus_2, up_z[1, 224:],
        pair_z[1, 224:], down_z[1, 224:], plus_6, up_z[0, 224:],
    ]
    ordered = lax.dynamic_slice(jnp.stack(steps + steps), ((8 - t) % 8, 0, 0), (8, 64, 128))

    pair_x = jnp.stack([rows, ring_step(rows, "x", 4, 2)])
    lat = call(latent_pack_kernel, struct((4, 656, 128), BF), [VM] * 6)(
        latent, one_back, two_back, stats_latent, gain_latent[None], shift_latent[None]
    )
    lat_all = lax.all_to_all(lat, "height", 0, 0, tiled=True)
    phased = cotangent.reshape(4, 4, 16, 2, 256).transpose(0, 1, 3, 2, 4)
    phased = after(phased, stats_latent)
    six = jnp.concatenate([phased, later(phased[:2], -1)], 0)
    cot_pair = jnp.stack([six, ring_step(six, "height", 4, 2)])
    pair_x = after(pair_x, lat_all, cot_pair)
    rest_x = ring_step(pair_x, "x", 4, 1)
    other_pair = swapped(pair_x)
    block_w = lax.all_gather(after(ordered, pair_x, up_w), ("x", "core", "height"))
    block_w = block_w.reshape(4, 2, 4, 8, 64, 128)

    cot_rest = ring_step(cot_pair, "height", 4, 1)
    other_rest = swapped(after(rest_x, cot_rest))

    refined = call(
        latent_conv_kernel,
        struct((4, 3, 8, 16, 128), BF),
        [SM, VM] + [HB] * 4,
        [
            pltpu.VMEM((3, 5, 10, 16, 512), BF),
            pltpu.VMEM((13824, 128), BF),
            pltpu.SemaphoreType.DMA,
        ],
    )(meta, lat_all, *[in_hbm(v) for v in (pair_x, rest_x, other_pair, other_rest)])
    refined_all = lax.all_to_all(refined, "height", 0, 0, tiled=True)

    cot_t = call(transpose_kernel, struct((4, 256, 512), BF), [SM, VM, VM])(meta, cot_pair, cot_rest)
    grad_active, weight = call(
        grad_active_kernel,
        [struct((512, 256), F32), struct((8, 864, 256), BF)],
        [SM, VM, VM, HB],
        [
            pltpu.VMEM((6, 6, 4, 16, 256), BF),
            pltpu.VMEM((2, 4, 8, 16, 128), BF),
            pltpu.SemaphoreType.DMA,
        ],
    )(meta, after(cot_pair, cot_t), cot_rest, block_w)
    weight = weight.reshape(6912, 256)

    up, up_sums = call(
        upsample_kernel,
        [struct((3, 2, 8, 2, 2, 16, 256), BF), struct((8, 8, 256), F32)],
        [VM, HB],
        [pltpu.VMEM((512, 2048), BF), pltpu.SemaphoreType.DMA],
    )(refined_all, up_w)
    up = up.reshape(6, 16, 2, 16, 256)
    stats_block = lax.all_to_all(up_sums, "tm", 0, 0, tiled=True)

    gn, grad_sums = call(
        grad_norm_kernel, [struct((512, 256), F32), struct((4, 8, 256), F32)], [SM] + [VM] * 5
    )(meta, up, stats_block, gain2, shift2, grad_active)
    all_sums = lax.all_to_all(grad_sums, "height", 0, 0, tiled=True)

    gw, q = call(
        weight_grad_kernel,
        [struct((8, 72, 256), BF), struct((6, 18, 4, 16, 256), BF)],
        [SM] + [VM] * 5,
        [pltpu.VMEM((2304, 256), F32)],
    )(meta, up, stats_block, gain2, shift2, cot_t)
    packed = call(pack_kernel, struct((8, 80, 256), BF), [VM] * 2)(gw, all_sums)
    got = lax.all_to_all(packed, "tm", 0, 0, tiled=True)

    decoded = call(
        decode_kernel,
        struct((4, 4, 32, 256), BF),
        [SM] + [VM] * 3,
        [pltpu.VMEM((2, 16, 32, 128), F32)],
    )(meta, up, q, weight)

    grad_up, grad_weight, totals = call(
        final_kernel,
        [struct((4, 4, 32, 256), BF), struct((72, 256), F32), struct((8, 256), F32)],
        [SM] + [VM] * 6,
        [pltpu.VMEM((2, 16, 32, 128), F32)],
    )(meta, up, stats_block, gain2, got, gn, cotangent)
    return decoded, grad_up, grad_weight, totals[1], totals[0]


def solution(mesh):
    fine = Mesh(
        mesh.devices.reshape(4, 2, 2, 8, 4), ("x", "zh", "core", "tm", "height")
    )
    dp = ("x", "zh", "core")
    return jax.shard_map(
        local,
        mesh=fine,
        in_specs=(
            P((*dp, "tm"), None, None, "height"),
            P("height"),
            P("height"),
            P("tm", "height"),
            P("height", None),
            P(),
            P(),
            P(("tm", "height"), None),
            P((*dp, "tm"), "height", None, None),
        ),
        out_specs=(
            P((*dp, "tm"), "height", None, None),
            P((*dp, "tm"), "height", None, None),
            P((*dp, "tm", "height"), None),
            P(dp),
            P(dp),
        ),
        check_vma=False,
    )
```
